32 devices in a mesh: expert: 4 (over z), dp: 2 (over y), tensor: 4 (over x, core).
Axes of the slice: x: 2, y: 2, z: 4, core: 2. Of those that a mesh axis runs over, the one named last changes fastest.
Arguments:
- tokens: bfloat16 [1024, 4096], P(('expert', 'dp')), may hold values from -6 to 6
- out_grad: bfloat16 [1024, 4096], P(('expert', 'dp')), may hold values from -1.1953125 to 1.1953125
- expert_index: int32 [1024, 2], P(('expert', 'dp')), may hold values from 0 to 3, as said below
- slot_index: int32 [1024, 2], P(('expert', 'dp')), may hold values from 0 to 95, as said below
- gate_probs: float32 [1024, 2], P(('expert', 'dp')), may hold values from 0.05 to 0.95
- gate_weight: bfloat16 [4, 4096, 2048], P('expert', None, 'tensor'), may hold values from -0.09375 to 0.09375
- up_weight: bfloat16 [4, 4096, 2048], P('expert', None, 'tensor'), may hold values from -0.09375 to 0.09375
- down_weight: bfloat16 [4, 2048, 4096], P('expert', 'tensor'), may hold values from -0.125 to 0.125
Outputs:
- token_grad: bfloat16 [1024, 4096], P(('expert', 'dp'), 'tensor')
- gate_grad: bfloat16 [4, 4096, 2048], P('expert', 'dp', 'tensor')
- up_grad: bfloat16 [4, 4096, 2048], P('expert', 'dp', 'tensor')
- down_grad: bfloat16 [4, 2048, 4096], P('expert', 'tensor', 'dp')
The draws below stay inside these ranges and needn't reach their ends.
Inputs may be any that keep to these rules, and one draw needn't show every extreme that they name: `expert_index`: in each block of 128 rows (the rows of one device) the two experts of a row differ; in every block one expert is named by exactly 96 rows and no expert by more, and that expert is the same for all blocks of one group. `slot_index`: within one block, the choices that name one expert carry distinct slots that run from 0 to their number minus one; a choice whose slot is 48 or more is dropped.
All inputs are finite; a program needn't handle non-finite values.
Results may differ from the reference program's by a relative error of at most 0.014.
Values may be sent and summed in bfloat16 or wider, within the bound.
A program may use at most 64 MiB of HBM per device.

```python
import jax
import jax.numpy as jnp
from jax import lax

D = 4096
FF = 2048
TOK_DEV = 128
EXPERTS = 4
CAP = 48
GROUPS = 2
ROWS = 192
TOKENS = 1024
N_EXPERT = 4


def route_block(block_key, hot_expert):
    most_rows = min(2 * CAP, TOK_DEV)
    subkeys = jax.random.split(block_key, 5)
    expert_bias = jax.random.randint(subkeys[0], (EXPERTS, 1), 0, 512)
    cell_noise = jax.random.randint(subkeys[1], (EXPERTS, most_rows), 0, 1024)
    cell_count = EXPERTS * most_rows
    cell_index = jnp.arange(cell_count, dtype=jnp.int32).reshape(EXPERTS, most_rows)
    cell_score = (expert_bias + cell_noise) * cell_count + cell_index
    cell_owner = jnp.arange(EXPERTS, dtype=jnp.int32)[:, None] + 0 * cell_index
    cell_score = jnp.where(cell_owner == hot_expert, cell_score + 4194304, cell_score)
    picked = lax.top_k(cell_score.reshape(-1), 2 * TOK_DEV)[1]
    labels = jnp.sort(cell_owner.reshape(-1)[picked])
    tie_break = jax.random.randint(subkeys[2], (2 * TOK_DEV,), 0, 1024) * (2 * TOK_DEV) + jnp.arange(2 * TOK_DEV, dtype=jnp.int32)
    same_expert = labels[:, None] == labels[None, :]
    slot_value = jnp.sum(same_expert & (tie_break[None, :] < tie_break[:, None]), axis=1).astype(jnp.int32)
    token_order = jax.random.permutation(subkeys[3], TOK_DEV).astype(jnp.int32)
    column_flip = jax.random.randint(subkeys[4], (TOK_DEV,), 0, 2)
    pick_index = jnp.arange(2 * TOK_DEV, dtype=jnp.int32)
    token_of = token_order[pick_index % TOK_DEV]
    column = (pick_index // TOK_DEV + column_flip[token_of]) % 2
    expert_table = jnp.zeros((TOK_DEV, 2), jnp.int32).at[token_of, column].set(labels)
    slot_table = jnp.zeros((TOK_DEV, 2), jnp.int32).at[token_of, column].set(slot_value)
    return (expert_table, slot_table)


def route_all(key):
    base_key = jax.random.fold_in(key, 4242)
    hot_expert = jax.random.randint(jax.random.fold_in(base_key, 1), (GROUPS,), 0, EXPERTS)
    blocks = jnp.arange(TOKENS // TOK_DEV, dtype=jnp.int32)
    block_keys = jax.vmap(lambda block: jax.random.fold_in(base_key, block + 2))(blocks)
    expert_table, slot_table = jax.vmap(route_block)(block_keys, hot_expert[blocks % GROUPS])
    return (expert_table.reshape(TOKENS, 2), slot_table.reshape(TOKENS, 2))


def draw_expert_index(key, part):
    return route_all(key)[0]


def draw_slot_index(key, part):
    return route_all(key)[1]


def shard_levels(key, shape, pieces, low, largest):
    gain, own = 1.0, jax.random.fold_in(key, 6)
    for dim, blocks in pieces:
        steps = jnp.exp(jax.random.uniform(jax.random.fold_in(own, dim), (blocks,), jnp.float32, low / len(pieces), largest / len(pieces)))
        gain = gain * jnp.repeat(steps, shape[dim] // blocks).reshape([-1 if axis == dim else 1 for axis in range(len(shape))])
    return gain


def centred(rng, dims, width, bound, cuts=(), held_as=jnp.bfloat16):
    entries = jax.random.normal(rng, dims, jnp.float32) * width
    if len(cuts) > 0:
        entries = shard_levels(rng, dims, cuts, -0.22, 0.18) * entries
    return jnp.clip(entries, min=-bound, max=bound).astype(held_as)


def setup_inputs(seed: int = 0) -> dict:
    keys = jax.random.split(jax.random.key(seed), 9)
    return {
        "tokens": centred(keys[0], (TOKENS, D), 1.0, 6.0, ((0, 8),)),
        "out_grad": centred(keys[1], (TOKENS, D), 0.2, 1.1953125, ((0, 8),)),
        "expert_index": draw_expert_index(jax.random.fold_in(keys[8], 71), 0),
        "slot_index": draw_slot_index(jax.random.fold_in(keys[8], 71), 0),
        "gate_probs": jnp.clip(0.05 + 0.9 * jax.random.uniform(keys[4], (TOKENS, 2), jnp.float32) ** shard_levels(keys[4], (TOKENS, 2), ((0, 8),), -0.2, 0.2), 0.05, 0.95),
        "gate_weight": centred(keys[5], (EXPERTS, D, FF), D ** -0.5, 0.09375, ((0, 4), (2, 4))),
        "up_weight": centred(keys[6], (EXPERTS, D, FF), D ** -0.5, 0.09375, ((0, 4), (2, 4))),
        "down_weight": centred(keys[7], (EXPERTS, FF, D), FF ** -0.5, 0.125, ((0, 4), (1, 4))),
    }


def reference(tokens, out_grad, expert_index, slot_index, gate_probs, gate_weight, up_weight, down_weight):
    row_index = jnp.arange(TOKENS, dtype=jnp.int32)
    block_index = row_index // TOK_DEV
    group_of = block_index % GROUPS
    source_of = block_index // GROUPS
    total_slots = GROUPS * EXPERTS * ROWS
    kept_mask = slot_index < CAP
    position = ((group_of[:, None] * EXPERTS + expert_index) * N_EXPERT + source_of[:, None]) * CAP + slot_index
    position = jnp.where(kept_mask, position, total_slots).astype(jnp.int32)
    flat_position = position.reshape(-1)
    owners = jnp.repeat(row_index, 2)
    source_row = jnp.full((total_slots + 1,), TOKENS, jnp.int32).at[flat_position].set(owners)[:total_slots]
    source_row = source_row.reshape(GROUPS, EXPERTS, ROWS)
    slot_prob = jnp.zeros((total_slots + 1,), jnp.float32).at[flat_position].set(gate_probs.reshape(-1).astype(jnp.float32))[:total_slots]
    slot_prob = slot_prob.reshape(GROUPS, EXPERTS, ROWS)
    padded_tokens = jnp.concatenate([tokens, jnp.zeros((1, D), tokens.dtype)], axis=0)
    padded_grads = jnp.concatenate([out_grad, jnp.zeros((1, D), out_grad.dtype)], axis=0)
    contract_last = (((1,), (1,)), ((), ()))
    contract_first = (((0,), (0,)), ((), ()))

    def expert_pass(expert):
        gate_matrix = gate_weight[expert]
        up_matrix = up_weight[expert]
        down_matrix = down_weight[expert]

        def group_pass(group_index):
            picked = source_row[group_index, expert]
            routed = padded_tokens[picked]
            scaled = (slot_prob[group_index, expert][:, None] * padded_grads[picked].astype(jnp.float32)).astype(jnp.bfloat16)
            gate_value = jnp.dot(routed, gate_matrix, preferred_element_type=jnp.float32)
            up_value = jnp.dot(routed, up_matrix, preferred_element_type=jnp.float32)
            gate_sigmoid = jax.nn.sigmoid(gate_value)
            activated = gate_value * gate_sigmoid
            hidden = (activated * up_value).astype(jnp.bfloat16)
            back_grad = lax.dot_general(scaled, down_matrix, contract_last, preferred_element_type=jnp.float32)
            gate_delta = (back_grad * up_value * gate_sigmoid * (1.0 + gate_value * (1.0 - gate_sigmoid))).astype(jnp.bfloat16)
            up_delta = (back_grad * activated).astype(jnp.bfloat16)
            slot_grad = lax.dot_general(gate_delta, gate_matrix, contract_last, preferred_element_type=jnp.float32)
            slot_grad = slot_grad + lax.dot_general(up_delta, up_matrix, contract_last, preferred_element_type=jnp.float32)
            part_gate = lax.dot_general(routed, gate_delta, contract_first, preferred_element_type=jnp.float32).astype(jnp.bfloat16)
            part_up = lax.dot_general(routed, up_delta, contract_first, preferred_element_type=jnp.float32).astype(jnp.bfloat16)
            part_down = lax.dot_general(hidden, scaled, contract_first, preferred_element_type=jnp.float32).astype(jnp.bfloat16)
            return slot_grad, part_gate, part_up, part_down

        slot_grad, part_gate, part_up, part_down = lax.map(group_pass, jnp.arange(GROUPS, dtype=jnp.int32))
        gate_total = jnp.sum(part_gate.astype(jnp.float32), axis=0).astype(jnp.bfloat16)
        up_total = jnp.sum(part_up.astype(jnp.float32), axis=0).astype(jnp.bfloat16)
        down_total = jnp.sum(part_down.astype(jnp.float32), axis=0).astype(jnp.bfloat16)
        return slot_grad, gate_total, up_total, down_total

    slot_grad, gate_grad, up_grad, down_grad = lax.map(expert_pass, jnp.arange(EXPERTS, dtype=jnp.int32))
    flat_grad = jnp.transpose(slot_grad, (1, 0, 2, 3)).reshape(total_slots, D)
    safe_position = jnp.minimum(position, total_slots - 1).astype(jnp.int32)
    chosen = jnp.where(kept_mask[:, :, None], flat_grad[safe_position], jnp.zeros((), flat_grad.dtype))
    token_grad = jnp.sum(chosen, axis=1).astype(jnp.bfloat16)
    return (token_grad, gate_grad, up_grad, down_grad)
```

```python
import functools

import jax
import jax.numpy as jnp
from jax import lax
from jax.experimental import pallas as pl
from jax.experimental.pallas import tpu as pltpu
from jax.sharding import PartitionSpec as P

MESH = pl.DeviceIdType.MESH
LAST = (((1,), (1,)), ((), ()))
FIRST = (((0,), (0,)), ((), ()))


def greet(sizes):
    experts = sizes
    e = lax.axis_index("expert")
    g = lax.axis_index("dp")
    t = lax.axis_index("tensor")
    sib = t + 1 - 2 * lax.rem(t, 2)
    opp = lax.rem(t + 2, 4)
    barrier = pltpu.get_barrier_semaphore()
    partners = [(e, g, sib), (e, g, opp), (e, 1 - g, t)]
    partners += [(lax.rem(e + d, experts), g, t) for d in range(1, experts)]
    for who in partners:
        pl.semaphore_signal(barrier, inc=1, device_id=who, device_id_type=MESH)
    return e, g, t, partners, barrier


def one_hot(ei, si, k, capacity, slots):
    exp = ei[:, k : k + 1]
    slot = si[:, k : k + 1]
    target = jnp.where(slot < capacity, exp * capacity + slot, slots)
    place = lax.broadcasted_iota(jnp.int32, (ei.shape[0], slots), 1)
    return jnp.where(place == target, 1.0, 0.0).astype(jnp.bfloat16)


def dispatch_kernel(
    experts, tok, grd, ei, si, prob, got, oth, send,
    z_s, z_r, x_s, x_r, b_s, b_r, y_s, y_r, o_s, o_r
):
    e, g, t, partners, barrier = greet(experts)
    sib, opp, other = partners[:3]
    slots, width = send.shape[2], send.shape[3]
    half = tok.shape[1] // 2
    capacity = slots // experts

    first = one_hot(ei[...], si[...], 0, capacity, slots)
    second = one_hot(ei[...], si[...], 1, capacity, slots)
    both = first + second
    for h in range(2):
        cols = pl.ds(pl.multiple_of(h * half + t * width, width), width)
        send[0, h] = lax.dot_general(
            both, tok[:, cols], FIRST, preferred_element_type=jnp.float32
        ).astype(jnp.bfloat16)
        cot = grd[:, cols].astype(jnp.float32)
        send[1, h] = (
            lax.dot_general(
                first, (prob[:, 0:1] * cot).astype(jnp.bfloat16), FIRST,
                preferred_element_type=jnp.float32,
            )
            + lax.dot_general(
                second, (prob[:, 1:2] * cot).astype(jnp.bfloat16), FIRST,
                preferred_element_type=jnp.float32,
            )
        ).astype(jnp.bfloat16)
    pl.semaphore_wait(barrier, len(partners))

    def rows(s):
        return pl.ds(pl.multiple_of(s * capacity, 16), capacity)

    def window(q):
        return pl.ds(pl.multiple_of(q * width, width), width)

    mine, across = window(t), window(opp[2])
    sends, recvs = [], []

    def remote(src, dst, s_sem, r_sem, who):
        copy = pltpu.make_async_remote_copy(
            src_ref=src, dst_ref=dst, send_sem=s_sem, recv_sem=r_sem,
            device_id=who, device_id_type=MESH,
        )
        copy.start()
        sends.append(copy)
        return copy

    z, x = {}, {}
    for a in range(2):
        for d in (2, 3, 1):
            if d < experts:
                z[d, a] = remote(
                    send.at[a, :, rows(lax.rem(e + d, experts))],
                    got.at[a, :, rows(e), mine],
                    z_s.at[d, a], z_r.at[d, a], partners[2 + d],
                )
    for a in range(2):
        for h in range(2):
            got[a, h, rows(e), mine] = send[a, h, rows(e)]
    for d in (0, 1, 3, 2):
        block = rows(lax.rem(e + experts - d, experts))
        for a in range(2):
            if d:
                z[d, a].wait_recv()
            here = got.at[a, :, block, mine]
            x[d, a] = remote(here, here, x_s.at[d, a], x_r.at[d, a], opp)
            recvs.append(remote(here, here, b_s.at[d, a, 0], b_r.at[d, a, 0], sib))
    y = {}
    for a in range(2):
        y[a, 0] = remote(
            got.at[a, 1 - g, :, mine], oth.at[a, :, mine],
            y_s.at[a, 0], y_r.at[a, 0], other,
        )
    for d in (0, 1, 3, 2):
        block = rows(lax.rem(e + experts - d, experts))
        for a in range(2):
            x[d, a].wait_recv()
            here = got.at[a, :, block, across]
            recvs.append(remote(here, here, b_s.at[d, a, 1], b_r.at[d, a, 1], sib))
    for a in range(2):
        y[a, 1] = remote(
            got.at[a, 1 - g, :, across], oth.at[a, :, across],
            y_s.at[a, 1], y_r.at[a, 1], other,
        )
    for i in range(2):
        for a in range(2):
            y[a, i].wait_recv()
            here = oth.at[a, :, across if i else mine]
            recvs.append(remote(here, here, o_s.at[a, i], o_r.at[a, i], sib))
    for copy in recvs:
        copy.wait_recv()
    for copy in sends:
        copy.wait_send()


def return_kernel(
    experts, delta, wg, wu, ei, si, out, oth, part, near, far_out, far, total, back,
    y_s, y_r, b_s, b_r, x_s, x_r, z_s, z_r
):
    e, g, t, partners, barrier = greet(experts)
    sib, opp, other = partners[:3]
    slots, width = back.shape
    capacity = slots // experts
    tile = 512
    c = lax.rem(t, 2)
    xi = t // 2
    sends = []

    def remote(src, dst, s_sem, r_sem, who):
        copy = pltpu.make_async_remote_copy(
            src_ref=src, dst_ref=dst, send_sem=s_sem, recv_sem=r_sem,
            device_id=who, device_id_type=MESH,
        )
        copy.start()
        sends.append(copy)
        return copy

    def product(q):
        @pl.loop(0, width // tile)
        def _(i):
            block = pl.ds(pl.multiple_of(q * width + i * tile, tile), tile)
            value = lax.dot_general(
                delta[0], wg[block, :], LAST, preferred_element_type=jnp.float32
            ) + lax.dot_general(
                delta[1], wu[block, :], LAST, preferred_element_type=jnp.float32
            )
            part[q, :, pl.ds(pl.multiple_of(i * tile, tile), tile)] = value.astype(jnp.bfloat16)

    def rows(s):
        return pl.ds(pl.multiple_of(s * capacity, 16), capacity)

    pl.semaphore_wait(barrier, len(partners))
    y = [
        remote(delta.at[k], oth.at[k], y_s.at[k], y_r.at[k], other) for k in range(3)
    ]
    q_far, q_near = (1 - xi) * 2, xi * 2
    product(q_far + 1 - c)
    b_far = remote(part.at[q_far + 1 - c], near.at[0], b_s.at[0], b_r.at[0], sib)
    product(q_far + c)
    b_far.wait_recv()
    order = (2, 3, 1, 0)
    x = {}
    for d in order:
        block = rows(lax.rem(e + d, experts))
        far_out[block] = (
            part[q_far + c, block].astype(jnp.float32) + near[0, block].astype(jnp.float32)
        ).astype(jnp.bfloat16)
        x[d] = remote(far_out.at[block], far.at[block], x_s.at[d], x_r.at[d], opp)
    product(q_near + 1 - c)
    b_near = remote(part.at[q_near + 1 - c], near.at[1], b_s.at[1], b_r.at[1], sib)
    product(q_near + c)
    b_near.wait_recv()
    z = {}
    for d in order:
        who = lax.rem(e + d, experts)
        block = rows(who)
        x[d].wait_recv()
        value = (
            part[q_near + c, block].astype(jnp.float32)
            + near[1, block].astype(jnp.float32)
            + far[block].astype(jnp.float32)
        ).astype(jnp.bfloat16)
        if d:
            total[block] = value
            z[d] = remote(total.at[block], back.at[rows(e)], z_s.at[d], z_r.at[d], partners[2 + d])
        else:
            back[block] = value
    pick = one_hot(ei[...], si[...], 0, capacity, slots) + one_hot(
        ei[...], si[...], 1, capacity, slots
    )
    for d in (1, 3, 2):
        z[d].wait_recv()
    out[...] = jnp.dot(pick, back[...], preferred_element_type=jnp.float32).astype(jnp.bfloat16)
    for copy in y:
        copy.wait_recv()
    for copy in sends:
        copy.wait_send()


VMEM = pl.BlockSpec(memory_space=pltpu.VMEM)
DMA = pltpu.SemaphoreType.DMA


def params(identity):
    return pltpu.CompilerParams(
        collective_id=identity, has_side_effects=True, vmem_limit_bytes=48 * 1024 * 1024
    )


def fast_on_device(
    tokens, out_grad, expert_index, slot_index, gate_probs, gate_weight, up_weight, down_weight
):
    local_rows, model_width = tokens.shape
    experts = lax.axis_size("expert")
    slots = 3 * local_rows // 2
    hidden_part = gate_weight.shape[2]
    half = model_width // 2
    width = half // lax.axis_size("tensor")
    share = model_width // lax.axis_size("tensor")
    bf = jnp.bfloat16
    got, oth = pl.pallas_call(
        functools.partial(dispatch_kernel, experts),
        out_shape=(
            jax.ShapeDtypeStruct((2, 2, slots, half), bf),
            jax.ShapeDtypeStruct((2, slots, half), bf),
        ),
        in_specs=[VMEM] * 5,
        out_specs=(VMEM, VMEM),
        scratch_shapes=[
            pltpu.VMEM((2, 2, slots, width), bf),
            DMA((experts, 2)), DMA((experts, 2)),
            DMA((experts, 2)), DMA((experts, 2)),
            DMA((experts, 2, 2)), DMA((experts, 2, 2)),
            DMA((2, 2)), DMA((2, 2)),
            DMA((2, 2)), DMA((2, 2)),
        ],
        compiler_params=params(0),
        name="dispatch",
    )(tokens, out_grad, expert_index, slot_index, gate_probs)
    gate_matrix, up_matrix, down_matrix = gate_weight[0], up_weight[0], down_weight[0]

    def forward(rows, matrix):
        return sum(
            jnp.dot(rows[h], matrix[h * half : (h + 1) * half], preferred_element_type=jnp.float32)
            for h in range(2)
        )

    gate_value = forward(got[0], gate_matrix)
    up_value = forward(got[0], up_matrix)
    back_grad = sum(
        lax.dot_general(
            got[1, h], down_matrix[:, h * half : (h + 1) * half], LAST,
            preferred_element_type=jnp.float32,
        )
        for h in range(2)
    )
    gate_sigmoid = jax.nn.sigmoid(gate_value)
    activated = gate_value * gate_sigmoid
    hidden = (activated * up_value).astype(bf)
    gate_delta = (
        back_grad * up_value * gate_sigmoid * (1.0 + gate_value * (1.0 - gate_sigmoid))
    ).astype(bf)
    up_delta = (back_grad * activated).astype(bf)
    delta = jnp.stack([gate_delta, up_delta, hidden])
    token_grad, delta_oth = pl.pallas_call(
        functools.partial(return_kernel, experts),
        out_shape=(
            jax.ShapeDtypeStruct((local_rows, share), bf),
            jax.ShapeDtypeStruct((3, slots, hidden_part), bf),
        ),
        in_specs=[VMEM] * 5,
        out_specs=(VMEM, VMEM),
        scratch_shapes=[
            pltpu.VMEM((4, slots, share), bf),
            pltpu.VMEM((2, slots, share), bf),
            pltpu.VMEM((slots, share), bf),
            pltpu.VMEM((slots, share), bf),
            pltpu.VMEM((slots, share), bf),
            pltpu.VMEM((slots, share), bf),
            DMA((3,)), DMA((3,)),
            DMA((2,)), DMA((2,)),
            DMA((experts,)), DMA((experts,)),
            DMA((experts,)), DMA((experts,)),
        ],
        compiler_params=params(1),
        name="giveback",
    )(delta, gate_matrix, up_matrix, expert_index, slot_index)

    def grads_kernel(got_ref, oth_ref, delta_ref, delta_oth_ref, gg, ug, dg):
        g = lax.axis_index("dp")
        i = pl.program_id(0)
        n = gg.shape[0]
        cols = pl.ds(pl.multiple_of(i * n, n), n)

        def both(a_own, a_oth, b_own, b_oth):
            return (
                lax.dot_general(a_own, b_own, FIRST, preferred_element_type=jnp.float32)
                + lax.dot_general(a_oth, b_oth, FIRST, preferred_element_type=jnp.float32)
            ).astype(bf)

        tok_own, tok_oth = got_ref[0, g, :, cols], oth_ref[0, :, cols]
        gg[...] = both(tok_own, tok_oth, delta_ref[0], delta_oth_ref[0])
        ug[...] = both(tok_own, tok_oth, delta_ref[1], delta_oth_ref[1])
        dg[...] = both(delta_ref[2], delta_oth_ref[2], got_ref[1, g, :, cols], oth_ref[1, :, cols])

    tile = 512
    gate_grad, up_grad, down_grad = pl.pallas_call(
        grads_kernel,
        grid=(half // tile,),
        out_shape=(
            jax.ShapeDtypeStruct((half, hidden_part), bf),
            jax.ShapeDtypeStruct((half, hidden_part), bf),
            jax.ShapeDtypeStruct((hidden_part, half), bf),
        ),
        in_specs=[VMEM] * 4,
        out_specs=(
            pl.BlockSpec((tile, hidden_part), lambda i: (i, 0)),
            pl.BlockSpec((tile, hidden_part), lambda i: (i, 0)),
            pl.BlockSpec((hidden_part, tile), lambda i: (0, i)),
        ),
        compiler_params=pltpu.CompilerParams(vmem_limit_bytes=48 * 1024 * 1024),
        name="weight_grads",
    )(got, oth, delta, delta_oth)
    return (token_grad, gate_grad[None], up_grad[None], down_grad[None])


def on_device(
    tokens, out_grad, expert_index, slot_index, gate_probs, gate_weight, up_weight, down_weight
):
    local_rows, model_width = tokens.shape
    experts = lax.axis_size("expert")
    capacity = 3 * local_rows // (2 * experts)
    slot_count = experts * capacity
    kept_mask = slot_index < capacity
    target = jnp.where(kept_mask, expert_index * capacity + slot_index, slot_count)
    owners = jnp.repeat(jnp.arange(local_rows, dtype=jnp.int32), 2)
    source_row = (
        jnp.full((slot_count + 1,), local_rows, jnp.int32)
        .at[target.reshape(-1)]
        .set(owners)[:slot_count]
    )
    slot_prob = (
        jnp.zeros((slot_count + 1,), jnp.float32)
        .at[target.reshape(-1)]
        .set(gate_probs.reshape(-1))[:slot_count]
    )
    send_tokens = jnp.take(tokens, source_row, axis=0, mode="fill", fill_value=0)
    send_grads = (
        slot_prob[:, None] * jnp.take(out_grad, source_row, axis=0, mode="fill", fill_value=0)
    ).astype(jnp.bfloat16)
    tensor_part = model_width // lax.axis_size("tensor")
    offset = lax.axis_index("tensor") * tensor_part
    token_share = lax.dynamic_slice_in_dim(send_tokens, offset, tensor_part, 1)
    grad_share = lax.dynamic_slice_in_dim(send_grads, offset, tensor_part, 1)
    token_share, grad_share = (
        lax.all_to_all(token_share, "expert", split_axis=0, concat_axis=0, tiled=True),
        lax.all_to_all(grad_share, "expert", split_axis=0, concat_axis=0, tiled=True),
    )
    routed, scaled = (
        lax.all_gather(token_share, "tensor", axis=1, tiled=True),
        lax.all_gather(grad_share, "tensor", axis=1, tiled=True),
    )
    gate_matrix = gate_weight[0]
    up_matrix = up_weight[0]
    down_matrix = down_weight[0]
    contract_last = (((1,), (1,)), ((), ()))
    gate_value = jnp.dot(routed, gate_matrix, preferred_element_type=jnp.float32)
    up_value = jnp.dot(routed, up_matrix, preferred_element_type=jnp.float32)
    gate_sigmoid = jax.nn.sigmoid(gate_value)
    activated = gate_value * gate_sigmoid
    hidden = (activated * up_value).astype(jnp.bfloat16)
    back_grad = lax.dot_general(
        scaled, down_matrix, contract_last, preferred_element_type=jnp.float32
    )
    gate_delta = (
        back_grad * up_value * gate_sigmoid * (1.0 + gate_value * (1.0 - gate_sigmoid))
    ).astype(jnp.bfloat16)
    up_delta = (back_grad * activated).astype(jnp.bfloat16)
    gate_rows = gate_matrix
    up_rows = up_matrix
    gate_term = lax.dot_general(
        gate_rows, gate_delta, contract_last, preferred_element_type=jnp.float32
    )
    summed = lax.psum_scatter(
        gate_term
        + lax.dot_general(up_rows, up_delta, contract_last, preferred_element_type=jnp.float32),
        "tensor",
        scatter_dimension=0,
        tiled=True,
    )
    returned = lax.all_to_all(
        summed.reshape(tensor_part, experts, capacity),
        "expert",
        split_axis=1,
        concat_axis=1,
        tiled=True,
    )
    slot_rows = jnp.transpose(returned.reshape(tensor_part, slot_count))
    safe_target = jnp.minimum(target, slot_count - 1)
    chosen = jnp.take(slot_rows, safe_target.reshape(-1), axis=0).reshape(
        local_rows, 2, tensor_part
    )
    chosen = jnp.where(kept_mask[:, :, None], chosen, jnp.zeros((), jnp.float32))
    token_grad = jnp.sum(chosen, axis=1).astype(jnp.bfloat16)
    hidden_part = gate_matrix.shape[1]
    width_share = model_width // lax.axis_size("dp")
    token_cols, grad_cols = (
        lax.all_to_all(routed, "dp", split_axis=1, concat_axis=0, tiled=True),
        lax.all_to_all(scaled, "dp", split_axis=1, concat_axis=0, tiled=True),
    )
    rows_each = routed.shape[0]

    def rounded_sum(left, right, form):
        product = jnp.einsum(form, left, right, preferred_element_type=jnp.float32)
        return jnp.sum(
            lax.optimization_barrier(product.astype(jnp.bfloat16)).astype(jnp.float32), axis=0
        )

    piece_gate = lax.all_gather(gate_delta, "dp", axis=0, tiled=True)
    piece_up = lax.all_gather(up_delta, "dp", axis=0, tiled=True)
    piece_hidden = lax.all_gather(hidden, "dp", axis=0, tiled=True)
    length = piece_gate.shape[0]
    groups = length // rows_each
    token_rows = token_cols.reshape(groups, rows_each, width_share)
    grad_rows = grad_cols.reshape(groups, rows_each, width_share)
    gate_rows = piece_gate.reshape(groups, rows_each, hidden_part)
    up_rows = piece_up.reshape(groups, rows_each, hidden_part)
    hidden_rows = piece_hidden.reshape(groups, rows_each, hidden_part)
    gate_sum = rounded_sum(token_rows, gate_rows, "nrk,nrf->nkf")
    up_sum = rounded_sum(token_rows, up_rows, "nrk,nrf->nkf")
    down_sum = rounded_sum(hidden_rows, grad_rows, "nrf,nrk->nfk")
    gate_grad = gate_sum.astype(jnp.bfloat16)
    up_grad = up_sum.astype(jnp.bfloat16)
    down_grad = down_sum.astype(jnp.bfloat16)
    return (token_grad, gate_grad[None], up_grad[None], down_grad[None])


def solution(mesh):
    sizes = dict(mesh.shape)

    def body(*args):
        local_rows, model_width = args[0].shape
        capacity = 3 * local_rows // (2 * sizes["expert"])
        fits = (
            sizes["expert"] == 4
            and sizes["dp"] == 2
            and sizes["tensor"] == 4
            and capacity % 16 == 0
            and model_width % 4096 == 0
            and args[5].shape[2] % 256 == 0
        )
        return fast_on_device(*args) if fits else on_device(*args)

    return jax.shard_map(
        body,
        mesh=mesh,
        in_specs=(
            P(("expert", "dp"), None),
            P(("expert", "dp"), None),
            P(("expert", "dp"), None),
            P(("expert", "dp"), None),
            P(("expert", "dp"), None),
            P("expert", None, "tensor"),
            P("expert", None, "tensor"),
            P("expert", "tensor", None),
        ),
        out_specs=(
            P(("expert", "dp"), "tensor"),
            P("expert", "dp", "tensor"),
            P("expert", "dp", "tensor"),
            P("expert", "tensor", "dp"),
        ),
        check_vma=False,
    )
```

```python
import functools

import jax
import jax.numpy as jnp
from jax import lax
from jax.experimental import pallas as pl
from jax.experimental.pallas import tpu as pltpu
from jax.sharding import PartitionSpec as P

MESH = pl.DeviceIdType.MESH
LAST = (((1,), (1,)), ((), ()))
FIRST = (((0,), (0,)), ((), ()))


def greet(sizes):
    experts = sizes
    e = lax.axis_index("expert")
    g = lax.axis_index("dp")
    t = lax.axis_index("tensor")
    sib = t + 1 - 2 * lax.rem(t, 2)
    opp = lax.rem(t + 2, 4)
    barrier = pltpu.get_barrier_semaphore()
    partners = [(e, g, sib), (e, g, opp), (e, 1 - g, t)]
    partners += [(lax.rem(e + d, experts), g, t) for d in range(1, experts)]
    for who in partners:
        pl.semaphore_signal(barrier, inc=1, device_id=who, device_id_type=MESH)
    return e, g, t, partners, barrier


def one_hot(ei, si, k, capacity, slots):
    exp = ei[k : k + 1, :]
    slot = si[k : k + 1, :]
    target = jnp.where(slot < capacity, exp * capacity + slot, slots)
    place = lax.broadcasted_iota(jnp.int32, (slots, ei.shape[1]), 0)
    return place == target


def layer_kernel(
    experts, tok_hbm, grd_hbm, wg_hbm, wu_hbm, wd_hbm, ei, si, prob,
    out, own, oth, delta, delta_oth,
    tok, grd, wg, wu, wd, send, got, gate, up, back_grad,
    part, near, far_out, far, total, back,
    l_s, w_s, z_s, z_r, x_s, x_r, b_s, b_r, y_s, y_r, o_s, o_r,
    dy_s, dy_r, n_s, n_r, f_s, f_r, r_s, r_r
):
    e, g, t, partners, barrier = greet(experts)
    sib, opp, other = partners[:3]
    slots, width = send.shape[2], send.shape[3]
    half = got.shape[3]
    share = 2 * width
    capacity = slots // experts
    order = (0, 1, 3, 2)

    def window(q):
        return pl.ds(pl.multiple_of(q * width, width), width)

    def wide(h, q):
        return pl.ds(pl.multiple_of(h * half + q * width, width), width)

    def rows(s):
        return pl.ds(pl.multiple_of(s * capacity, 16), capacity)

    loads = []
    for h in range(2):
        loads.append(pltpu.make_async_copy(tok_hbm.at[:, wide(h, t)], tok.at[h], l_s.at[0, h]))
        loads.append(pltpu.make_async_copy(grd_hbm.at[:, wide(h, t)], grd.at[h], l_s.at[1, h]))
    for copy in loads:
        copy.start()
    weights = [
        pltpu.make_async_copy(wg_hbm.at[0], wg, w_s.at[0]),
        pltpu.make_async_copy(wu_hbm.at[0], wu, w_s.at[1]),
        pltpu.make_async_copy(wd_hbm.at[0], wd, w_s.at[2]),
    ]
    first = one_hot(ei[...], si[...], 0, capacity, slots)
    second = one_hot(ei[...], si[...], 1, capacity, slots)
    both = jnp.where(first | second, 1.0, 0.0).astype(jnp.bfloat16)
    prob_row = prob[...]
    slot_prob = jnp.sum(
        jnp.where(first, prob_row[0:1], 0.0) + jnp.where(second, prob_row[1:2], 0.0),
        axis=1, keepdims=True,
    )
    for copy in loads:
        copy.wait()
    for h in range(2):
        send[0, h] = jnp.dot(both, tok[h], preferred_element_type=jnp.float32).astype(jnp.bfloat16)
        send[1, h] = (
            slot_prob * jnp.dot(both, grd[h], preferred_element_type=jnp.float32)
        ).astype(jnp.bfloat16)
    pl.semaphore_wait(barrier, len(partners))

    mine, across = window(t), window(opp[2])
    sends, recvs = [], []

    def remote(src, dst, s_sem, r_sem, who):
        copy = pltpu.make_async_remote_copy(
            src_ref=src, dst_ref=dst, send_sem=s_sem, recv_sem=r_sem,
            device_id=who, device_id_type=MESH,
        )
        copy.start()
        sends.append(copy)
        return copy

    z, x, b, y = {}, {}, {}, {}
    for a in range(2):
        for d in (2, 3, 1):
            z[d, a] = remote(
                send.at[a, :, rows(lax.rem(e + d, experts))],
                got.at[a, :, rows(e), mine],
                z_s.at[d, a], z_r.at[d, a], partners[2 + d],
            )
    for a in range(2):
        for h in range(2):
            got[a, h, rows(e), mine] = send[a, h, rows(e)]
    for copy in weights:
        copy.start()

    def spread(d, a, i):
        block = rows(lax.rem(e + experts - d, experts))
        cols = across if i else mine
        here = got.at[a, :, block, cols]
        if i == 0:
            if d:
                z[d, a].wait_recv()
            x[d, a] = remote(here, here, x_s.at[d, a], x_r.at[d, a], opp)
        else:
            x[d, a].wait_recv()
        b[d, a, i] = remote(here, here, b_s.at[d, a, i], b_r.at[d, a, i], sib)
        y[d, a, i] = remote(
            got.at[a, 1 - g, block, cols], oth.at[a, block, cols],
            y_s.at[d, a, i], y_r.at[d, a, i], other,
        )

    def near_sum(q, start):
        for ref, w in ((gate, wg), (up, wu)):
            value = sum(
                jnp.dot(
                    got[0, h, :, window(q)], w[wide(h, q), :], preferred_element_type=jnp.float32
                )
                for h in range(2)
            )
            ref[...] = value if start else ref[...] + value

    def back_sum(q, start):
        value = sum(
            lax.dot_general(
                got[1, h, :, window(q)], wd[:, wide(h, q)], LAST,
                preferred_element_type=jnp.float32,
            )
            for h in range(2)
        )
        back_grad[...] = value if start else back_grad[...] + value

    spread(0, 0, 0)
    spread(0, 1, 0)
    for d in order[1:]:
        spread(d, 0, 0)
    spread(0, 0, 1)
    for prev, d in zip(order[:3], order[1:]):
        spread(d, 1, 0)
        spread(d, 0, 1)
    weights[0].wait()
    weights[1].wait()
    near_sum(t, True)
    spread(0, 1, 1)
    for d in order:
        b[d, 0, 0].wait_recv()
    near_sum(sib[2], False)
    spread(1, 1, 1)
    near_sum(opp[2], False)
    for d in order:
        b[d, 0, 1].wait_recv()
    near_sum(lax.rem(sib[2] + 2, 4), False)
    spread(3, 1, 1)
    weights[2].wait()
    back_sum(t, True)
    for d in order:
        b[d, 1, 0].wait_recv()
    back_sum(sib[2], False)
    spread(2, 1, 1)
    back_sum(opp[2], False)
    for d in order:
        b[d, 1, 1].wait_recv()
    back_sum(lax.rem(sib[2] + 2, 4), False)

    keep = pltpu.make_async_copy(got.at[:, g], own, l_s.at[0, 0])
    keep.start()
    v, u, k = gate[...], up[...], back_grad[...]
    sig = jax.nn.sigmoid(v)
    act = v * sig
    delta[0] = (k * u * sig * (1.0 + v * (1.0 - sig))).astype(jnp.bfloat16)
    delta[1] = (k * act).astype(jnp.bfloat16)
    delta[2] = (act * u).astype(jnp.bfloat16)

    dy = [
        remote(delta.at[i], delta_oth.at[i], dy_s.at[i], dy_r.at[i], other) for i in range(3)
    ]
    tile = width
    c = lax.rem(t, 2)
    xi = t // 2

    def product(q):
        @pl.loop(0, share // tile)
        def _(i):
            block = pl.ds(pl.multiple_of(q * share + i * tile, tile), tile)
            value = lax.dot_general(
                delta[0], wg[block, :], LAST, preferred_element_type=jnp.float32
            ) + lax.dot_general(
                delta[1], wu[block, :], LAST, preferred_element_type=jnp.float32
            )
            part[q, :, pl.ds(pl.multiple_of(i * tile, tile), tile)] = value.astype(jnp.bfloat16)

    q_far, q_near = (1 - xi) * 2, xi * 2
    product(q_far + 1 - c)
    b_far = remote(part.at[q_far + 1 - c], near.at[0], n_s.at[0], n_r.at[0], sib)
    product(q_far + c)
    b_far.wait_recv()
    back_order = (2, 3, 1, 0)
    f = {}
    for d in back_order:
        block = rows(lax.rem(e + d, experts))
        far_out[block] = (
            part[q_far + c, block].astype(jnp.float32) + near[0, block].astype(jnp.float32)
        ).astype(jnp.bfloat16)
        f[d] = remote(far_out.at[block], far.at[block], f_s.at[d], f_r.at[d], opp)
    product(q_near + 1 - c)
    b_near = remote(part.at[q_near + 1 - c], near.at[1], n_s.at[1], n_r.at[1], sib)
    product(q_near + c)
    b_near.wait_recv()
    r = {}
    for d in back_order:
        block = rows(lax.rem(e + d, experts))
        f[d].wait_recv()
        value = (
            part[q_near + c, block].astype(jnp.float32)
            + near[1, block].astype(jnp.float32)
            + far[block].astype(jnp.float32)
        ).astype(jnp.bfloat16)
        if d:
            total[block] = value
            r[d] = remote(total.at[block], back.at[rows(e)], r_s.at[d], r_r.at[d], partners[2 + d])
        else:
            back[block] = value
    for a in range(2):
        for i in range(2):
            for d in order:
                y[d, a, i].wait_recv()
            here = oth.at[a, :, across if i else mine]
            recvs.append(remote(here, here, o_s.at[a, i], o_r.at[a, i], sib))
    keep.wait()
    for d in (1, 3, 2):
        r[d].wait_recv()
    out[...] = lax.dot_general(
        both, back[...], FIRST, preferred_element_type=jnp.float32
    ).astype(jnp.bfloat16)
    for copy in recvs:
        copy.wait_recv()
    for copy in dy:
        copy.wait_recv()
    for copy in sends:
        copy.wait_send()


VMEM = pl.BlockSpec(memory_space=pltpu.VMEM)
HBM = pl.BlockSpec(memory_space=pltpu.HBM)
DMA = pltpu.SemaphoreType.DMA


def fast_on_device(
    tokens, out_grad, expert_index, slot_index, gate_probs, gate_weight, up_weight, down_weight
):
    local_rows, model_width = tokens.shape
    experts = lax.axis_size("expert")
    slots = 3 * local_rows // 2
    hidden_part = gate_weight.shape[2]
    half = model_width // 2
    width = half // lax.axis_size("tensor")
    share = model_width // lax.axis_size("tensor")
    bf = jnp.bfloat16
    token_grad, got, oth, delta, delta_oth = pl.pallas_call(
        functools.partial(layer_kernel, experts),
        out_shape=(
            jax.ShapeDtypeStruct((local_rows, share), bf),
            jax.ShapeDtypeStruct((2, slots, half), bf),
            jax.ShapeDtypeStruct((2, slots, half), bf),
            jax.ShapeDtypeStruct((3, slots, hidden_part), bf),
            jax.ShapeDtypeStruct((3, slots, hidden_part), bf),
        ),
        in_specs=[HBM] * 5 + [VMEM] * 3,
        out_specs=(VMEM,) * 5,
        scratch_shapes=[
            pltpu.VMEM((2, local_rows, width), bf),
            pltpu.VMEM((2, local_rows, width), bf),
            pltpu.VMEM((model_width, hidden_part), bf),
            pltpu.VMEM((model_width, hidden_part), bf),
            pltpu.VMEM((hidden_part, model_width), bf),
            pltpu.VMEM((2, 2, slots, width), bf),
            pltpu.VMEM((2, 2, slots, half), bf),
            pltpu.VMEM((slots, hidden_part), jnp.float32),
            pltpu.VMEM((slots, hidden_part), jnp.float32),
            pltpu.VMEM((slots, hidden_part), jnp.float32),
            pltpu.VMEM((4, slots, share), bf),
            pltpu.VMEM((2, slots, share), bf),
            pltpu.VMEM((slots, share), bf),
            pltpu.VMEM((slots, share), bf),
            pltpu.VMEM((slots, share), bf),
            pltpu.VMEM((slots, share), bf),
            DMA((2, 2)), DMA((3,)),
            DMA((experts, 2)), DMA((experts, 2)),
            DMA((experts, 2)), DMA((experts, 2)),
            DMA((experts, 2, 2)), DMA((experts, 2, 2)),
            DMA((experts, 2, 2)), DMA((experts, 2, 2)),
            DMA((2, 2)), DMA((2, 2)),
            DMA((3,)), DMA((3,)),
            DMA((2,)), DMA((2,)),
            DMA((experts,)), DMA((experts,)),
            DMA((experts,)), DMA((experts,)),
        ],
        compiler_params=pltpu.CompilerParams(
            collective_id=0, has_side_effects=True, vmem_limit_bytes=54 * 1024 * 1024
        ),
        name="layer",
    )(
        tokens, out_grad, gate_weight, up_weight, down_weight,
        expert_index.T, slot_index.T, gate_probs.T,
    )

    def grads_kernel(got_ref, oth_ref, delta_ref, delta_oth_ref, gg, ug, dg):
        i = pl.program_id(0)
        n = gg.shape[0]
        cols = pl.ds(pl.multiple_of(i * n, n), n)

        def both(a_own, a_oth, b_own, b_oth):
            return (
                lax.dot_general(a_own, b_own, FIRST, preferred_element_type=jnp.float32)
                + lax.dot_general(a_oth, b_oth, FIRST, preferred_element_type=jnp.float32)
            ).astype(bf)

        tok_own, tok_oth = got_ref[0, :, cols], oth_ref[0, :, cols]
        gg[...] = both(tok_own, tok_oth, delta_ref[0], delta_oth_ref[0])
        ug[...] = both(tok_own, tok_oth, delta_ref[1], delta_oth_ref[1])
        dg[...] = both(delta_ref[2], delta_oth_ref[2], got_ref[1, :, cols], oth_ref[1, :, cols])

    tile = 512
    gate_grad, up_grad, down_grad = pl.pallas_call(
        grads_kernel,
        grid=(half // tile,),
        out_shape=(
            jax.ShapeDtypeStruct((half, hidden_part), bf),
            jax.ShapeDtypeStruct((half, hidden_part), bf),
            jax.ShapeDtypeStruct((hidden_part, half), bf),
        ),
        in_specs=[VMEM] * 4,
        out_specs=(
            pl.BlockSpec((tile, hidden_part), lambda i: (i, 0)),
            pl.BlockSpec((tile, hidden_part), lambda i: (i, 0)),
            pl.BlockSpec((hidden_part, tile), lambda i: (0, i)),
        ),
        compiler_params=pltpu.CompilerParams(vmem_limit_bytes=48 * 1024 * 1024),
        name="weight_grads",
    )(got, oth, delta, delta_oth)
    return (token_grad, gate_grad[None], up_grad[None], down_grad[None])


def on_device(
    tokens, out_grad, expert_index, slot_index, gate_probs, gate_weight, up_weight, down_weight
):
    local_rows, model_width = tokens.shape
    experts = lax.axis_size("expert")
    capacity = 3 * local_rows // (2 * experts)
    slot_count = experts * capacity
    kept_mask = slot_index < capacity
    target = jnp.where(kept_mask, expert_index * capacity + slot_index, slot_count)
    owners = jnp.repeat(jnp.arange(local_rows, dtype=jnp.int32), 2)
    source_row = (
        jnp.full((slot_count + 1,), local_rows, jnp.int32)
        .at[target.reshape(-1)]
        .set(owners)[:slot_count]
    )
    slot_prob = (
        jnp.zeros((slot_count + 1,), jnp.float32)
        .at[target.reshape(-1)]
        .set(gate_probs.reshape(-1))[:slot_count]
    )
    send_tokens = jnp.take(tokens, source_row, axis=0, mode="fill", fill_value=0)
    send_grads = (
        slot_prob[:, None] * jnp.take(out_grad, source_row, axis=0, mode="fill", fill_value=0)
    ).astype(jnp.bfloat16)
    tensor_part = model_width // lax.axis_size("tensor")
    offset = lax.axis_index("tensor") * tensor_part
    token_share = lax.dynamic_slice_in_dim(send_tokens, offset, tensor_part, 1)
    grad_share = lax.dynamic_slice_in_dim(send_grads, offset, tensor_part, 1)
    token_share, grad_share = (
        lax.all_to_all(token_share, "expert", split_axis=0, concat_axis=0, tiled=True),
        lax.all_to_all(grad_share, "expert", split_axis=0, concat_axis=0, tiled=True),
    )
    routed, scaled = (
        lax.all_gather(token_share, "tensor", axis=1, tiled=True),
        lax.all_gather(grad_share, "tensor", axis=1, tiled=True),
    )
    gate_matrix = gate_weight[0]
    up_matrix = up_weight[0]
    down_matrix = down_weight[0]
    contract_last = (((1,), (1,)), ((), ()))
    gate_value = jnp.dot(routed, gate_matrix, preferred_element_type=jnp.float32)
    up_value = jnp.dot(routed, up_matrix, preferred_element_type=jnp.float32)
    gate_sigmoid = jax.nn.sigmoid(gate_value)
    activated = gate_value * gate_sigmoid
    hidden = (activated * up_value).astype(jnp.bfloat16)
    back_grad = lax.dot_general(
        scaled, down_matrix, contract_last, preferred_element_type=jnp.float32
    )
    gate_delta = (
        back_grad * up_value * gate_sigmoid * (1.0 + gate_value * (1.0 - gate_sigmoid))
    ).astype(jnp.bfloat16)
    up_delta = (back_grad * activated).astype(jnp.bfloat16)
    gate_rows = gate_matrix
    up_rows = up_matrix
    gate_term = lax.dot_general(
        gate_rows, gate_delta, contract_last, preferred_element_type=jnp.float32
    )
    summed = lax.psum_scatter(
        gate_term
        + lax.dot_general(up_rows, up_delta, contract_last, preferred_element_type=jnp.float32),
        "tensor",
        scatter_dimension=0,
        tiled=True,
    )
    returned = lax.all_to_all(
        summed.reshape(tensor_part, experts, capacity),
        "expert",
        split_axis=1,
        concat_axis=1,
        tiled=True,
    )
    slot_rows = jnp.transpose(returned.reshape(tensor_part, slot_count))
    safe_target = jnp.minimum(target, slot_count - 1)
    chosen = jnp.take(slot_rows, safe_target.reshape(-1), axis=0).reshape(
        local_rows, 2, tensor_part
    )
    chosen = jnp.where(kept_mask[:, :, None], chosen, jnp.zeros((), jnp.float32))
    token_grad = jnp.sum(chosen, axis=1).astype(jnp.bfloat16)
    hidden_part = gate_matrix.shape[1]
    width_share = model_width // lax.axis_size("dp")
    token_cols, grad_cols = (
        lax.all_to_all(routed, "dp", split_axis=1, concat_axis=0, tiled=True),
        lax.all_to_all(scaled, "dp", split_axis=1, concat_axis=0, tiled=True),
    )
    rows_each = routed.shape[0]

    def rounded_sum(left, right, form):
        product = jnp.einsum(form, left, right, preferred_element_type=jnp.float32)
        return jnp.sum(
            lax.optimization_barrier(product.astype(jnp.bfloat16)).astype(jnp.float32), axis=0
        )

    piece_gate = lax.all_gather(gate_delta, "dp", axis=0, tiled=True)
    piece_up = lax.all_gather(up_delta, "dp", axis=0, tiled=True)
    piece_hidden = lax.all_gather(hidden, "dp", axis=0, tiled=True)
    length = piece_gate.shape[0]
    groups = length // rows_each
    token_rows = token_cols.reshape(groups, rows_each, width_share)
    grad_rows = grad_cols.reshape(groups, rows_each, width_share)
    gate_rows = piece_gate.reshape(groups, rows_each, hidden_part)
    up_rows = piece_up.reshape(groups, rows_each, hidden_part)
    hidden_rows = piece_hidden.reshape(groups, rows_each, hidden_part)
    gate_sum = rounded_sum(token_rows, gate_rows, "nrk,nrf->nkf")
    up_sum = rounded_sum(token_rows, up_rows, "nrk,nrf->nkf")
    down_sum = rounded_sum(hidden_rows, grad_rows, "nrf,nrk->nfk")
    gate_grad = gate_sum.astype(jnp.bfloat16)
    up_grad = up_sum.astype(jnp.bfloat16)
    down_grad = down_sum.astype(jnp.bfloat16)
    return (token_grad, gate_grad[None], up_grad[None], down_grad[None])


def solution(mesh):
    sizes = dict(mesh.shape)

    def body(*args):
        local_rows, model_width = args[0].shape
        capacity = 3 * local_rows // (2 * sizes["expert"])
        fits = (
            sizes["expert"] == 4
            and sizes["dp"] == 2
            and sizes["tensor"] == 4
            and capacity % 16 == 0
            and model_width % 4096 == 0
            and args[5].shape[2] % 256 == 0
        )
        return fast_on_device(*args) if fits else on_device(*args)

    return jax.shard_map(
        body,
        mesh=mesh,
        in_specs=(
            P(("expert", "dp"), None),
            P(("expert", "dp"), None),
            P(("expert", "dp"), None),
            P(("expert", "dp"), None),
            P(("expert", "dp"), None),
            P("expert", None, "tensor"),
            P("expert", None, "tensor"),
            P("expert", "tensor", None),
        ),
        out_specs=(
            P(("expert", "dp"), "tensor"),
            P("expert", "dp", "tensor"),
            P("expert", "dp", "tensor"),
            P("expert", "tensor", "dp"),
        ),
        check_vma=False,
    )
```
